256 devices in a mesh: dp: 16 (over x, y_lo, core), mp: 16 (over z, y_hi).
Axes of the slice: x: 4, y: 4 (y_hi: 2, y_lo: 2; y = y_hi * 2 + y_lo), z: 8, core: 2. Of those that a mesh axis runs over, the one named last changes fastest.
Arguments:
- block_input: bfloat16 [4096, 6144], P('dp'), may hold values from -6 to 6
- qkv_weight: bfloat16 [3, 6144, 4096], P(None, None, 'mp'), may hold values from -0.078125 to 0.078125
- grad_attn: bfloat16 [4096, 4096], P('dp', 'mp'), may hold values from -6 to 6
Outputs:
- grad_input: bfloat16 [4096, 6144], P('dp')
- grad_qkv: bfloat16 [3, 6144, 4096], P(None, 'dp', 'mp')
The draws below stay inside these ranges and needn't reach their ends.
All inputs are finite; a program needn't handle non-finite values.
Results may differ from the reference program's by a relative error of at most 0.025.
Values may be sent and summed in bfloat16 or wider, within the bound.
A program may use at most 128 MiB of HBM per device.

```python
import math
import jax
import jax.numpy as jnp
from jax import lax

D = 6144
HD = 128
PATCH = 256
INNER = 4096
TOKENS = 4096


def strengthened(drawn, rng, source, target, blocks, factor):
    owner, partner = [(jnp.arange(drawn.shape[axis_at]) // (drawn.shape[axis_at] // blocks)).reshape([-1 if axis == axis_at else 1 for axis in range(drawn.ndim)]) for axis_at in (source, target)]
    chosen = jax.random.permutation(rng, blocks)[partner]
    strong = (owner == chosen) | (owner == (partner + blocks // 2) % blocks)
    return jnp.where(strong, factor * drawn, drawn)


def levels(stream_key, dims, shards, smallest, top_value):
    factor_of = 1.0
    for axis_at, parts in shards:
        heights = jax.random.uniform(jax.random.fold_in(jax.random.fold_in(stream_key, 6), axis_at), (parts,), jnp.float32, smallest / len(shards), top_value / len(shards))
        factor_of = factor_of * jnp.repeat(jnp.exp(heights), dims[axis_at] // parts).reshape((-1,) + (1,) * (len(dims) - 1 - axis_at))
    return factor_of


def gaussian(key, extent, width, reach, pieces=(), held_as=jnp.bfloat16):
    gain = levels(key, extent, pieces, -0.22, 0.18) if pieces else 1.0
    result = jax.random.normal(key, extent, jnp.float32) * width * gain
    return jnp.minimum(jnp.maximum(result, -reach), reach).astype(held_as)


def bell_draw_with(rng, shape, deviation, reach, split, heavy, kind=jnp.bfloat16):
    result = deviation * jax.random.normal(rng, shape, jnp.float32)
    if split:
        result = result * levels(rng, shape, split, -0.22, 0.18)
    return jnp.clip(strengthened(result, jax.random.fold_in(rng, 3), *heavy), -reach, reach).astype(kind)


def setup_inputs(seed: int = 0) -> dict:
    keys = jax.random.split(jax.random.key(seed), 4)
    return {
        "block_input": bell_draw_with(keys[0], (TOKENS, D), 1.0, 6.0, ((0, 16),), (0, 1, 16, 2.0)),
        "qkv_weight": gaussian(keys[1], (3, D, INNER), D ** -0.5, 0.078125, ((2, 16),)),
        "grad_attn": gaussian(keys[2], (TOKENS, INNER), 1.0, 6.0, ((0, 16), (1, 16))),
    }


EPSILON = 1e-06

def normalize(values):
    row_mean = lax.optimization_barrier(jnp.mean(values, axis=-1, keepdims=True))
    centered = values - row_mean
    inv_std = lax.rsqrt(lax.optimization_barrier(jnp.mean(centered * centered, axis=-1, keepdims=True)) + EPSILON)
    return (centered * inv_std, inv_std)

def norm_back(upstream, normed, inv_std):
    mean_grad = lax.optimization_barrier(jnp.mean(upstream, axis=-1, keepdims=True))
    mean_cross = lax.optimization_barrier(jnp.mean(upstream * normed, axis=-1, keepdims=True))
    return inv_std * (upstream - mean_grad - normed * mean_cross)

def head_grads(normed_rows, qkv_weight, grad_attn):
    num_rows = normed_rows.shape[0]
    inner_width = qkv_weight.shape[2]
    frames = num_rows // PATCH
    num_heads = inner_width // HD
    factor = 1.0 / math.sqrt(HD)
    projected = jnp.einsum('td,cde->cte', normed_rows.astype(jnp.float32), qkv_weight.astype(jnp.float32)).astype(jnp.bfloat16)
    shaped = projected.reshape(3, frames, PATCH, num_heads, HD)
    q_hat, q_inv = normalize(shaped[0].astype(jnp.float32))
    k_hat, k_inv = normalize(shaped[1].astype(jnp.float32))
    q_low = q_hat.astype(jnp.bfloat16)
    k_low = k_hat.astype(jnp.bfloat16)
    scores = jnp.einsum('fqhd,fkhd->fhqk', q_low.astype(jnp.float32), k_low.astype(jnp.float32)) * factor
    exp_scores = jnp.exp(scores)
    attn_probs = exp_scores / lax.optimization_barrier(jnp.sum(exp_scores, axis=-1, keepdims=True))
    probs_low = attn_probs.astype(jnp.bfloat16)
    grad_out = grad_attn.reshape(frames, PATCH, num_heads, HD).astype(jnp.float32)
    values_low = shaped[2].astype(jnp.float32)
    grad_probs = jnp.einsum('fqhd,fkhd->fhqk', grad_out, values_low)
    grad_v = jnp.einsum('fhqk,fqhd->fkhd', probs_low.astype(jnp.float32), grad_out)
    row_term = lax.optimization_barrier(jnp.sum(attn_probs * grad_probs, axis=-1, keepdims=True))
    grad_scores = (attn_probs * (grad_probs - row_term) * factor).astype(jnp.bfloat16).astype(jnp.float32)
    grad_qhat = jnp.einsum('fhqk,fkhd->fqhd', grad_scores, k_low.astype(jnp.float32))
    grad_khat = jnp.einsum('fhqk,fqhd->fkhd', grad_scores, q_low.astype(jnp.float32))
    grad_q = norm_back(grad_qhat, q_hat, q_inv)
    grad_k = norm_back(grad_khat, k_hat, k_inv)
    stacked = jnp.stack([grad_q, grad_k, grad_v], axis=2)
    return stacked.reshape(num_rows, 3, inner_width).astype(jnp.bfloat16)

def reference(block_input, qkv_weight, grad_attn):
    x_hat, x_inv = normalize(block_input.astype(jnp.float32))
    normed = x_hat.astype(jnp.bfloat16)
    grad_proj = head_grads(normed, qkv_weight, grad_attn)
    grad_normed = jnp.einsum('tce,cde->td', grad_proj.astype(jnp.float32), qkv_weight.astype(jnp.float32))
    grad_input = norm_back(grad_normed, x_hat, x_inv).astype(jnp.bfloat16)
    grad_qkv = jnp.einsum('td,tce->cde', normed.astype(jnp.float32), grad_proj.astype(jnp.float32)).astype(jnp.bfloat16)
    return (grad_input, grad_qkv)
```

```python
import functools
import math

import jax
import jax.numpy as jnp
from jax import lax
from jax.experimental import pallas as pl
from jax.experimental.pallas import tpu as pltpu
from jax.sharding import PartitionSpec as P

MESH = pl.DeviceIdType.MESH
F32 = jnp.float32
BF16 = jnp.bfloat16
EPSILON = 1e-06

NX, NZ = 4, 8
ROWS = 256
D = 6144
HALF = D // 2
INNER = 256
HD = 128
OWN = 16
SLICE = 384
EH = 384


def normalize(values):
    row_mean = jnp.mean(values, axis=-1, keepdims=True)
    centered = values - row_mean
    inv_std = lax.rsqrt(jnp.mean(centered * centered, axis=-1, keepdims=True) + EPSILON)
    return centered * inv_std, inv_std


def norm_back(upstream, normed, inv_std):
    mean_grad = jnp.mean(upstream, axis=-1, keepdims=True)
    mean_cross = jnp.mean(upstream * normed, axis=-1, keepdims=True)
    return inv_std * (upstream - mean_grad - normed * mean_cross)


def dot(a, b, ca, cb):
    return lax.dot_general(a, b, (((ca,), (cb,)), ((), ())), preferred_element_type=F32)


def head_grads(q, k, v, g):
    factor = 1.0 / math.sqrt(HD)
    q_hat, q_inv = normalize(q.astype(F32))
    k_hat, k_inv = normalize(k.astype(F32))
    q_low = q_hat.astype(BF16)
    k_low = k_hat.astype(BF16)
    exp_scores = jnp.exp(dot(q_low, k_low, 1, 1) * factor)
    probs = exp_scores / jnp.sum(exp_scores, axis=-1, keepdims=True)
    grad_probs = dot(g, v, 1, 1)
    grad_v = dot(probs.astype(BF16), g, 0, 0)
    row_term = jnp.sum(probs * grad_probs, axis=-1, keepdims=True)
    grad_scores = (probs * (grad_probs - row_term) * factor).astype(BF16)
    grad_q = norm_back(dot(grad_scores, k_low, 1, 0), q_hat, q_inv)
    grad_k = norm_back(dot(grad_scores, q_low, 0, 0), k_hat, k_inv)
    return grad_q, grad_k, grad_v


def kernel(
    x_hbm, w_hbm, g_hbm, gi_hbm, gw_hbm,
    xv, wv, gv, nv, pv, gp, gp2, nr, tv, slots, ry, og, bp, rb, yb, xh, xinv, gwv,
    x_sem, w_sem, g_sem, o_sem, q_sem,
    core_s, core_r, rs_s, rs_r, ry_s, ry_r, ag_s, ag_r, ay_s, ay_r, b_s, b_r, by_s, by_r,
):
    dp, mp = lax.axis_index("dp"), lax.axis_index("mp")
    x, yl, c = dp // 4, (dp // 2) % 2, dp % 2
    z, yh = mp // 2, mp % 2

    def at(x_, yl_, c_, z_, yh_):
        return ((x_ * 2 + yl_) * 2 + c_, z_ * 2 + yh_)

    to_z = (at(x, yl, c, (z + 1) % NZ, yh), at(x, yl, c, (z + NZ - 1) % NZ, yh))
    to_x = (at((x + 1) % NX, yl, c, z, yh), at((x + NX - 1) % NX, yl, c, z, yh))
    to_yh = at(x, yl, c, z, 1 - yh)
    to_yl = at(x, 1 - yl, c, z, yh)
    to_core = at(x, yl, 1 - c, z, yh)

    x_copies = []
    for i in range(4):
        rows = pl.ds(i * 64, 64)
        x_copies.append(pltpu.make_async_copy(x_hbm.at[rows], xv.at[rows], x_sem.at[i]))
    w_copies = [pltpu.make_async_copy(w_hbm.at[i], wv.at[i], w_sem.at[i]) for i in range(3)]
    g_copy = pltpu.make_async_copy(g_hbm, gv, g_sem)
    for cp in x_copies + w_copies + [g_copy]:
        cp.start()

    barrier = pltpu.get_barrier_semaphore()
    neighbours = to_z + to_x + (to_yh, to_yl, to_core)
    for d in neighbours:
        pl.semaphore_signal(barrier, inc=1, device_id=d, device_id_type=MESH)

    sends = []

    def remote(src, dst, s, r, d):
        cp = pltpu.make_async_remote_copy(
            src_ref=src, dst_ref=dst, send_sem=s, recv_sem=r, device_id=d, device_id_type=MESH
        )
        cp.start()
        sends.append(cp)
        return cp

    for i in range(4):
        x_copies[i].wait()
        rows = pl.ds(i * 64, 64)
        nv[rows, :] = normalize(xv[rows, :].astype(F32))[0].astype(BF16)

    pl.semaphore_wait(barrier, len(neighbours))
    core = []
    for i in range(8):
        cols = pl.ds(pl.multiple_of((i * 2 + 1 - c) * SLICE, 128), SLICE)
        core.append(
            remote(nv.at[:, cols], nr.at[:, pl.ds(i * SLICE, SLICE)], core_s.at[i], core_r.at[i], to_core)
        )

    for i in range(3):
        w_copies[i].wait()
        pv[:, pl.ds(i * INNER, INNER)] = dot(nv[...], wv[i], 1, 0).astype(BF16)
    g_copy.wait()
    for h in range(2):
        cols = [pl.ds(i * INNER + h * HD, HD) for i in range(3)]
        grads = head_grads(pv[:, cols[0]], pv[:, cols[1]], pv[:, cols[2]], gv[:, pl.ds(h * HD, HD)])
        for col, grad in zip(cols, grads):
            gp[:, col] = grad.astype(BF16)
    core.append(remote(gp, gp2, core_s.at[8], core_r.at[8], to_core))

    def block_rows(block, j):
        h = 1 - yh if j == 0 else yh
        return pl.ds(pl.multiple_of(block * 2 * OWN + h * OWN, OWN), OWN)

    def rs_block(way, step):
        return (z + NZ - step - 1) % NZ if way == 0 else (z + step + 1) % NZ

    half = [pl.ds(0, HALF), pl.ds(HALF, HALF)]
    rs = {}

    def rs_send(way, step, j):
        src = (
            tv.at[block_rows(rs_block(way, 0), j), half[way]]
            if step == 0
            else slots.at[way, step - 1, j]
        )
        rs[way, step, j] = remote(
            src, slots.at[way, step, j], rs_s.at[way, step, j], rs_r.at[way, step, j], to_z[way]
        )

    def terms(cols):
        total = dot(gp[:, pl.ds(0, INNER)], wv[0, cols, :], 1, 1)
        for i in range(1, 3):
            total += dot(gp[:, pl.ds(i * INNER, INNER)], wv[i, cols, :], 1, 1)
        tv[:, cols] = total.astype(BF16)

    for way in range(2):
        def body(i, carry, way=way):
            terms(pl.ds(pl.multiple_of(way * HALF + i * 512, 512), 512))
            return carry

        lax.fori_loop(0, HALF // 512, body, 0)
        for j in range(2):
            rs_send(way, 0, j)

    def rs_take(step):
        for j in range(2):
            for way in range(2):
                rs[way, step, j].wait_recv()
                slot = slots.at[way, step, j]
                own = tv[block_rows(rs_block(way, step + 1), j), half[way]]
                slot[...] = (slot[...].astype(F32) + own.astype(F32)).astype(BF16)
                rs_send(way, step + 1, j)

    def b_units(k):
        for way in range(2):
            block = (x + NX - 1 - k) % NX if way == 0 else (x + 1 + k) % NX
            for j in range(2):
                ys = 1 - yl if j == 0 else yl
                mine = pl.ds(pl.multiple_of(((block * 2 + ys) * 2 + c) * SLICE, 128), SLICE)
                other = pl.ds(pl.multiple_of((block * 2 + ys) * SLICE, 128), SLICE)
                e = pl.ds(way * EH, EH)
                total = dot(nv[:, mine], gp[:, e], 0, 0) + dot(nr[:, other], gp2[:, e], 0, 0)
                bp[way, k, j] = total.astype(BF16)

    b = {}

    def b_send(way, step, j):
        src = bp.at[way, 0, j] if step == 0 else rb.at[way, step - 1, j]
        b[way, step, j] = remote(
            src, rb.at[way, step, j], b_s.at[way, step, j], b_r.at[way, step, j], to_x[way]
        )

    def b_sum(way, step, j):
        b[way, step, j].wait_recv()
        return rb[way, step, j].astype(F32) + bp[way, step + 1, j].astype(F32)

    def b_take(step):
        for j in range(2):
            for way in range(2):
                rb[way, step, j] = b_sum(way, step, j).astype(BF16)
                b_send(way, step + 1, j)

    for cp in core:
        cp.wait_recv()
    b_units(0)
    for j in range(2):
        for way in range(2):
            b_send(way, 0, j)
    own_rows = pl.ds(pl.multiple_of(mp * OWN, OWN), OWN)
    hat, inv = normalize(xv[own_rows, :].astype(F32))
    xh[...] = hat
    xinv[...] = jnp.broadcast_to(inv, xinv.shape)
    rs_take(0)
    b_units(1)
    rs_take(1)
    b_units(2)
    rs_take(2)
    b_units(3)
    rs_take(3)
    rs_take(4)
    b_take(0)
    rs_take(5)

    last = NZ - 2
    y = []
    for way in range(2):
        rs[way, last, 0].wait_recv()
        slot = slots.at[way, last, 0]
        own = tv[block_rows(z, 0), half[way]]
        slot[...] = (slot[...].astype(F32) + own.astype(F32)).astype(BF16)
        y.append(remote(slot, ry.at[way], ry_s.at[way], ry_r.at[way], to_yh))
    totals = []
    for way in range(2):
        rs[way, last, 1].wait_recv()
        y[way].wait_recv()
        own = tv[block_rows(z, 1), half[way]]
        totals.append(slots[way, last, 1].astype(F32) + own.astype(F32) + ry[way].astype(F32))
    grad_normed = jnp.concatenate(totals, axis=1)
    og[own_rows, :] = norm_back(grad_normed, xh[...], xinv[:, :1]).astype(BF16)

    ag = {}

    def ag_send(way, step, j):
        block = (z + NZ - step) % NZ if way == 0 else (z + step) % NZ
        part = og.at[block_rows(block, 1 - j), half[way]]
        ag[way, step, j] = remote(
            part, part, ag_s.at[way, step, j], ag_r.at[way, step, j], to_z[way]
        )

    def ag_take(step):
        for j in range(2):
            for way in range(2):
                ag[way, step, j].wait_recv()
                if step < NZ - 2:
                    ag_send(way, step + 1, j)

    ay = remote(og.at[own_rows, :], og.at[own_rows, :], ay_s, ay_r, to_yh)
    for way in range(2):
        ag_send(way, 0, 0)
    ay.wait_recv()
    for way in range(2):
        ag_send(way, 0, 1)
    ag_take(0)
    b_take(1)
    ag_take(1)
    ag_take(2)
    ag_take(3)
    by = []
    for way in range(2):
        rb[way, 2, 0] = b_sum(way, 2, 0).astype(BF16)
        by.append(remote(rb.at[way, 2, 0], yb.at[way], by_s.at[way], by_r.at[way], to_yl))
    ag_take(4)
    ag_take(5)
    for way in range(2):
        total = b_sum(way, 2, 1)
        by[way].wait_recv()
        total = (total + yb[way].astype(F32)).astype(BF16)
        if way == 0:
            gwv[0, :, :] = total[:, :256]
            gwv[1, :, :128] = total[:, 256:]
        else:
            gwv[1, :, 128:] = total[:, :128]
            gwv[2, :, :] = total[:, 128:]
    q_copy = pltpu.make_async_copy(gwv, gw_hbm, q_sem)
    q_copy.start()
    ag_take(6)
    o_copy = pltpu.make_async_copy(og, gi_hbm, o_sem)
    o_copy.start()
    for cp in sends:
        cp.wait_send()
    q_copy.wait()
    o_copy.wait()


def on_device(block_input, qkv_weight, grad_attn):
    dma = pltpu.SemaphoreType.DMA
    return pl.pallas_call(
        kernel,
        out_shape=(
            jax.ShapeDtypeStruct((ROWS, D), BF16),
            jax.ShapeDtypeStruct((3, SLICE, INNER), BF16),
        ),
        in_specs=[pl.BlockSpec(memory_space=pl.ANY)] * 3,
        out_specs=[pl.BlockSpec(memory_space=pl.ANY)] * 2,
        scratch_shapes=[
            pltpu.VMEM((ROWS, D), BF16),
            pltpu.VMEM((3, D, INNER), BF16),
            pltpu.VMEM((ROWS, INNER), BF16),
            pltpu.VMEM((ROWS, D), BF16),
            pltpu.VMEM((ROWS, 3 * INNER), BF16),
            pltpu.VMEM((ROWS, 3 * INNER), BF16),
            pltpu.VMEM((ROWS, 3 * INNER), BF16),
            pltpu.VMEM((ROWS, HALF), BF16),
            pltpu.VMEM((ROWS, D), BF16),
            pltpu.VMEM((2, NZ - 1, 2, OWN, HALF), BF16),
            pltpu.VMEM((2, OWN, HALF), BF16),
            pltpu.VMEM((ROWS, D), BF16),
            pltpu.VMEM((2, NX, 2, SLICE, EH), BF16),
            pltpu.VMEM((2, NX - 1, 2, SLICE, EH), BF16),
            pltpu.VMEM((2, SLICE, EH), BF16),
            pltpu.VMEM((OWN, D), F32),
            pltpu.VMEM((OWN, 128), F32),
            pltpu.VMEM((3, SLICE, INNER), BF16),
            dma((4,)), dma((3,)), dma(()), dma(()), dma(()),
            dma((9,)), dma((9,)),
            dma((2, NZ - 1, 2)), dma((2, NZ - 1, 2)),
            dma((2,)), dma((2,)),
            dma((2, NZ - 1, 2)), dma((2, NZ - 1, 2)),
            dma(()), dma(()),
            dma((2, NX - 1, 2)), dma((2, NX - 1, 2)),
            dma((2,)), dma((2,)),
        ],
        compiler_params=pltpu.CompilerParams(
            collective_id=0, has_side_effects=True, vmem_limit_bytes=56 * 2**20
        ),
        cost_estimate=pl.CostEstimate(flops=7_500_000_000, bytes_accessed=20_000_000, transcendentals=200_000),
    )(block_input, qkv_weight, grad_attn)


def solution(mesh):
    placed = (P("dp", None), P(None, None, "mp"), P("dp", "mp"))
    return jax.shard_map(
        on_device,
        mesh=mesh,
        in_specs=placed,
        out_specs=(P("dp", None), P(None, "dp", "mp")),
        check_vma=False,
    )
```

```python
import functools
import math

import jax
import jax.numpy as jnp
from jax import lax
from jax.experimental import pallas as pl
from jax.experimental.pallas import tpu as pltpu
from jax.sharding import PartitionSpec as P

MESH = pl.DeviceIdType.MESH
F32 = jnp.float32
BF16 = jnp.bfloat16
EPSILON = 1e-06

NX, NZ = 4, 8
ROWS = 256
D = 6144
HALF = D // 2
INNER = 256
HD = 128
OWN = 16
SLICE = 384
EH = 384
FRAME = ROWS // 2
RZ = 1536
XROWS = 64
TW = 512
AZ = 2048


def normalize(values):
    row_mean = jnp.mean(values, axis=-1, keepdims=True)
    centered = values - row_mean
    inv_std = lax.rsqrt(jnp.mean(centered * centered, axis=-1, keepdims=True) + EPSILON)
    return centered * inv_std, inv_std


def norm_back(upstream, normed, inv_std):
    mean_grad = jnp.mean(upstream, axis=-1, keepdims=True)
    mean_cross = jnp.mean(upstream * normed, axis=-1, keepdims=True)
    return inv_std * (upstream - mean_grad - normed * mean_cross)


def dot(a, b, ca, cb):
    return lax.dot_general(a, b, (((ca,), (cb,)), ((), ())), preferred_element_type=F32)


def head_grads(q, k, v, g):
    factor = 1.0 / math.sqrt(HD)
    q_hat, q_inv = normalize(q.astype(F32))
    k_hat, k_inv = normalize(k.astype(F32))
    q_low = q_hat.astype(BF16)
    k_low = k_hat.astype(BF16)
    exp_scores = jnp.exp(dot(q_low, k_low, 1, 1) * factor)
    probs = exp_scores / jnp.sum(exp_scores, axis=-1, keepdims=True)
    grad_probs = dot(g, v, 1, 1)
    grad_v = dot(probs.astype(BF16), g, 0, 0)
    row_term = jnp.sum(probs * grad_probs, axis=-1, keepdims=True)
    grad_scores = (probs * (grad_probs - row_term) * factor).astype(BF16)
    grad_q = norm_back(dot(grad_scores, k_low, 1, 0), q_hat, q_inv)
    grad_k = norm_back(dot(grad_scores, q_low, 0, 0), k_hat, k_inv)
    return grad_q, grad_k, grad_v


def kernel(
    x_hbm, w_hbm, g_hbm, og, gwv,
    xv, wv, gv, nv, pv, gp, gp2, nr, tv, slots, yx, ry, bp, rb, yb, xh, xinv,
    x_sem, w_sem, g_sem,
    core_s, core_r, rs_s, rs_r, yx_s, yx_r, ry_s, ry_r,
    ag_s, ag_r, ay_s, ay_r, b_s, b_r, by_s, by_r,
):
    dp, mp = lax.axis_index("dp"), lax.axis_index("mp")
    x, yl, c = dp // 4, (dp // 2) % 2, dp % 2
    z, yh = mp // 2, mp % 2

    def at(x_, yl_, c_, z_, yh_):
        return ((x_ * 2 + yl_) * 2 + c_, z_ * 2 + yh_)

    to_z = (at(x, yl, c, (z + 1) % NZ, yh), at(x, yl, c, (z + NZ - 1) % NZ, yh))
    to_x = (at((x + 1) % NX, yl, c, z, yh), at((x + NX - 1) % NX, yl, c, z, yh))
    to_yh = at(x, yl, c, z, 1 - yh)
    to_yl = at(x, 1 - yl, c, z, yh)
    to_core = at(x, yl, 1 - c, z, yh)

    def x_copy(i):
        rows = pl.ds(pl.multiple_of(i * XROWS, XROWS), XROWS)
        return pltpu.make_async_copy(x_hbm.at[rows], xv.at[rows], x_sem.at[i])

    def w_copy(i):
        return pltpu.make_async_copy(w_hbm.at[i], wv.at[i], w_sem.at[i])

    g_copy = pltpu.make_async_copy(g_hbm, gv, g_sem)
    for i in range(ROWS // XROWS):
        x_copy(i).start()
    for i in range(3):
        w_copy(i).start()
    g_copy.start()

    barrier = pltpu.get_barrier_semaphore()
    neighbours = to_z + to_x + (to_yh, to_yl, to_core)
    for d in neighbours:
        pl.semaphore_signal(barrier, inc=1, device_id=d, device_id_type=MESH)

    sends = []

    def remote(src, dst, s, r, d):
        cp = pltpu.make_async_remote_copy(
            src_ref=src, dst_ref=dst, send_sem=s, recv_sem=r, device_id=d, device_id_type=MESH
        )
        cp.start()
        sends.append(cp)
        return cp

    def loop(count, step):
        def body(i, carry):
            step(i)
            return carry

        lax.fori_loop(0, count, body, 0)

    def normed_rows(i):
        x_copy(i).wait()
        rows = pl.ds(pl.multiple_of(i * XROWS, XROWS), XROWS)
        shape = (XROWS, 128)
        tiles = [pl.ds(t * 128, 128) for t in range(D // 128)]
        total = jnp.zeros(shape, F32)
        for tile in tiles:
            total += xv[rows, tile].astype(F32)
        mean = jnp.broadcast_to(jnp.sum(total, axis=-1, keepdims=True) * (1.0 / D), shape)
        total = jnp.zeros(shape, F32)
        for tile in tiles:
            centered = xv[rows, tile].astype(F32) - mean
            total += centered * centered
        variance = jnp.sum(total, axis=-1, keepdims=True) * (1.0 / D)
        inv = jnp.broadcast_to(lax.rsqrt(variance + EPSILON), shape)
        for tile in tiles:
            nv[rows, tile] = ((xv[rows, tile].astype(F32) - mean) * inv).astype(BF16)

    loop(ROWS // XROWS, normed_rows)
    pl.semaphore_wait(barrier, len(neighbours))
    core = []
    for i in range(8):
        cols = pl.ds(pl.multiple_of((i * 2 + 1 - c) * SLICE, 128), SLICE)
        core.append(
            remote(nv.at[:, cols], nr.at[:, pl.ds(i * SLICE, SLICE)], core_s.at[i], core_r.at[i], to_core)
        )

    def project(i):
        w_copy(i).wait()
        pv[:, pl.ds(pl.multiple_of(i * INNER, INNER), INNER)] = dot(nv[...], wv[i], 1, 0).astype(BF16)

    loop(3, project)
    g_copy.wait()

    def head(h):
        start = pl.multiple_of(h * HD, HD)
        cols = [pl.ds(i * INNER + start, HD) for i in range(3)]
        grads = head_grads(pv[:, cols[0]], pv[:, cols[1]], pv[:, cols[2]], gv[:, pl.ds(start, HD)])
        for col, grad in zip(cols, grads):
            gp[:, col] = grad.astype(BF16)

    loop(INNER // HD, head)
    core.append(remote(gp, gp2, core_s.at[8], core_r.at[8], to_core))

    chains = [(way, ch) for ch in range(2) for way in range(2)]

    def hops(way, ch):
        return NZ // 2 if way == ch else NZ // 2 - 1

    def block_rows(block, h):
        return pl.ds(pl.multiple_of(h * FRAME + block * OWN, OWN), OWN)

    def ahead(way, far):
        return far if way == 0 else (NZ - far) % NZ

    rs_cols = [[pl.ds(ch * HALF, RZ)] * 2 + [pl.ds(ch * HALF + RZ, HALF - RZ)] for ch in range(2)]
    rs, y_first = {}, {}

    def rs_part(ch, delta, u, h):
        return tv.at[block_rows((z + delta) % NZ, h), rs_cols[ch][u]]

    def rs_own(ch, delta, u):
        own = rs_part(ch, delta, u, 1 - yh if u == 0 else yh)[...].astype(F32)
        if u == 2:
            y_first[ch, delta].wait_recv()
            own += yx[ch, delta].astype(F32)
        return own

    def rs_send(way, ch, k, u, src):
        rs[way, ch, k, u] = remote(
            src, slots.at[way, ch, k, u], rs_s.at[way, ch, k, u], rs_r.at[way, ch, k, u], to_z[way]
        )

    def rs_start(ch, u):
        for way in range(2):
            delta = ahead(way, hops(way, ch))
            if u == 2:
                yx[ch, delta] = rs_own(ch, delta, u).astype(BF16)
                src = yx.at[ch, delta]
            else:
                src = rs_part(ch, delta, u, 1 - yh if u == 0 else yh)
            rs_send(way, ch, 0, u, src)

    def rs_take(k, u):
        for way, ch in chains:
            far = hops(way, ch) - k - 1
            if far > 0:
                own = rs_own(ch, ahead(way, far), u)
                rs[way, ch, k, u].wait_recv()
                slots[way, ch, k, u] = (slots[way, ch, k, u].astype(F32) + own).astype(BF16)
                rs_send(way, ch, k + 1, u, slots.at[way, ch, k, u])

    def rs_total(ch, u):
        total = rs_own(ch, 0, u)
        for way in (1 - ch, ch):
            k = hops(way, ch) - 1
            rs[way, ch, k, u].wait_recv()
            total += slots[way, ch, k, u].astype(F32)
        return total

    def terms(start, width):
        def part(i):
            cols = pl.ds(pl.multiple_of(start + i * TW, TW), TW)
            total = dot(gp[:, pl.ds(0, INNER)], wv[0, cols, :], 1, 1)
            for j in range(1, 3):
                total += dot(gp[:, pl.ds(j * INNER, INNER)], wv[j, cols, :], 1, 1)
            tv[:, cols] = total.astype(BF16)

        loop(width // TW, part)

    for ch in range(2):
        terms(ch * HALF, RZ)
        for u in range(2):
            rs_start(ch, u)
    for ch in range(2):
        terms(ch * HALF + RZ, HALF - RZ)
    for delta in (4, 3, 5, 2, 6, 1, 7, 0):
        for ch in range(2):
            y_first[ch, delta] = remote(
                rs_part(ch, delta, 2, 1 - yh), yx.at[ch, delta], yx_s.at[ch, delta], yx_r.at[ch, delta], to_yh
            )

    def b_units(j):
        ys = 1 - yl if j == 0 else yl

        def unit(delta):
            block = (x + delta) % NX
            mine = pl.ds(pl.multiple_of(((block * 2 + ys) * 2 + c) * SLICE, 128), SLICE)
            other = pl.ds(pl.multiple_of((block * 2 + ys) * SLICE, 128), SLICE)
            total = dot(nv[:, mine], gp[...], 0, 0) + dot(nr[:, other], gp2[...], 0, 0)
            for ch in range(2):
                bp[j, delta, ch] = total[:, ch * EH : (ch + 1) * EH].astype(BF16)

        loop(NX, unit)

    b = {}

    def b_send(way, ch, k, j, src):
        b[way, ch, k, j] = remote(
            src, rb.at[way, ch, k, j], b_s.at[way, ch, k, j], b_r.at[way, ch, k, j], to_x[way]
        )

    def b_start(j):
        for way in range(2):
            b_send(way, way, 0, j, bp.at[j, 2, way])
        for way in range(2):
            b_send(way, 1 - way, 0, j, bp.at[j, 1 if way == 0 else 3, 1 - way])

    def b_take(j):
        for way in range(2):
            b[way, way, 0, j].wait_recv()
            own = bp[j, 1 if way == 0 else 3, way].astype(F32)
            rb[way, way, 0, j] = (rb[way, way, 0, j].astype(F32) + own).astype(BF16)
            b_send(way, way, 1, j, rb.at[way, way, 0, j])

    def b_total(ch, j):
        b[1 - ch, ch, 0, j].wait_recv()
        b[ch, ch, 1, j].wait_recv()
        total = bp[j, 0, ch].astype(F32) + rb[1 - ch, ch, 0, j].astype(F32)
        return total + rb[ch, ch, 1, j].astype(F32)

    for cp in core:
        cp.wait_recv()
    b_units(0)
    b_start(0)
    own_rows = block_rows(z, yh)
    hat, inv = normalize(xv[own_rows, :].astype(F32))
    xh[...] = hat
    xinv[...] = jnp.broadcast_to(inv, xinv.shape)
    rs_take(0, 0)
    rs_take(0, 1)
    for ch in range(2):
        rs_start(ch, 2)
    b_units(1)
    rs_take(1, 0)
    rs_take(1, 1)
    rs_take(0, 2)
    b_take(0)
    b_start(1)
    rs_take(2, 0)
    rs_take(2, 1)
    rs_take(1, 2)
    y = []
    for ch in range(2):
        slots[ch, ch, 3, 0] = rs_total(ch, 0).astype(BF16)
        y.append(remote(slots.at[ch, ch, 3, 0], ry.at[ch], ry_s.at[ch], ry_r.at[ch], to_yh))
    rs_take(2, 2)
    totals = [[rs_total(ch, 1)] for ch in range(2)]
    for ch in range(2):
        totals[ch].append(rs_total(ch, 2))
    for ch in range(2):
        y[ch].wait_recv()
        totals[ch][0] += ry[ch].astype(F32)
    grad_normed = jnp.concatenate(totals[0] + totals[1], axis=1)
    og[own_rows, :] = norm_back(grad_normed, xh[...], xinv[:, :1]).astype(BF16)

    ag, ay = {}, {}
    ag_cols = [[pl.ds(ch * HALF, HALF), pl.ds(ch * HALF, AZ)] for ch in range(2)]
    y_cols = [pl.ds(ch * HALF + AZ, HALF - AZ) for ch in range(2)]

    def ag_send(way, ch, k, u):
        block = (z + ahead(1 - way, k)) % NZ
        part = og.at[block_rows(block, yh if u == 0 else 1 - yh), ag_cols[ch][u]]
        ag[way, ch, k, u] = remote(
            part, part, ag_s.at[way, ch, k, u], ag_r.at[way, ch, k, u], to_z[way]
        )

    def y_send(ch, delta, cols, i):
        part = og.at[block_rows((z + delta) % NZ, yh), cols]
        ay[ch, i] = remote(part, part, ay_s.at[ch, i], ay_r.at[ch, i], to_yh)

    def ag_take(k):
        for u in range(2):
            for way, ch in ((0, 0), (1, 1), (1, 0), (0, 1)):
                if k < hops(way, ch):
                    ag[way, ch, k, u].wait_recv()
                    if k + 1 < hops(way, ch):
                        ag_send(way, ch, k + 1, u)
                    if u == 0:
                        delta = ahead(1 - way, k + 1)
                        y_send(ch, delta, y_cols[ch], delta)

    for ch in range(2):
        y_send(ch, 0, ag_cols[ch][1], NZ)
    for ch in range(2):
        for way in range(2):
            ag_send(way, ch, 0, 0)
    for ch in range(2):
        y_send(ch, 0, y_cols[ch], 0)
    for ch in range(2):
        ay[ch, NZ].wait_recv()
        for way in range(2):
            ag_send(way, ch, 0, 1)
    by = []
    for ch in range(2):
        rb[ch, ch, 1, 0] = b_total(ch, 0).astype(BF16)
        by.append(remote(rb.at[ch, ch, 1, 0], yb.at[ch], by_s.at[ch], by_r.at[ch], to_yl))
    ag_take(0)
    b_take(1)
    ag_take(1)
    ag_take(2)
    for ch in range(2):
        total = b_total(ch, 1)
        by[ch].wait_recv()
        total = (total + yb[ch].astype(F32)).astype(BF16)
        if ch == 0:
            gwv[0, :, :] = total[:, :256]
            gwv[1, :, :128] = total[:, 256:]
        else:
            gwv[1, :, 128:] = total[:, :128]
            gwv[2, :, :] = total[:, 128:]
    ag_take(3)
    for i in range(NZ):
        for ch in range(2):
            ay[ch, i].wait_recv()
    for cp in sends:
        cp.wait_send()


def on_device(block_input, qkv_weight, grad_attn):
    dma = pltpu.SemaphoreType.DMA
    vmem = pl.BlockSpec(memory_space=pltpu.VMEM)
    return pl.pallas_call(
        kernel,
        out_shape=(pltpu.VMEM((ROWS, D), BF16), pltpu.VMEM((3, SLICE, INNER), BF16)),
        in_specs=[pl.BlockSpec(memory_space=pl.ANY)] * 3,
        out_specs=(vmem, vmem),
        scratch_shapes=[
            pltpu.VMEM((ROWS, D), BF16),
            pltpu.VMEM((3, D, INNER), BF16),
            pltpu.VMEM((ROWS, INNER), BF16),
            pltpu.VMEM((ROWS, D), BF16),
            pltpu.VMEM((ROWS, 3 * INNER), BF16),
            pltpu.VMEM((ROWS, 3 * INNER), BF16),
            pltpu.VMEM((ROWS, 3 * INNER), BF16),
            pltpu.VMEM((ROWS, HALF), BF16),
            pltpu.VMEM((ROWS, D), BF16),
            pltpu.VMEM((2, 2, NZ // 2, 3, OWN, RZ), BF16),
            pltpu.VMEM((2, NZ, OWN, HALF - RZ), BF16),
            pltpu.VMEM((2, OWN, RZ), BF16),
            pltpu.VMEM((2, NX, 2, SLICE, EH), BF16),
            pltpu.VMEM((2, 2, 2, 2, SLICE, EH), BF16),
            pltpu.VMEM((2, SLICE, EH), BF16),
            pltpu.VMEM((OWN, D), F32),
            pltpu.VMEM((OWN, 128), F32),
            dma((ROWS // XROWS,)), dma((3,)), dma(()),
            dma((9,)), dma((9,)),
            dma((2, 2, NZ // 2, 3)), dma((2, 2, NZ // 2, 3)),
            dma((2, NZ)), dma((2, NZ)),
            dma((2,)), dma((2,)),
            dma((2, 2, NZ // 2, 2)), dma((2, 2, NZ // 2, 2)),
            dma((2, NZ + 1)), dma((2, NZ + 1)),
            dma((2, 2, 2, 2)), dma((2, 2, 2, 2)),
            dma((2,)), dma((2,)),
        ],
        compiler_params=pltpu.CompilerParams(
            collective_id=0, has_side_effects=True, vmem_limit_bytes=54 * 2**20
        ),
        cost_estimate=pl.CostEstimate(flops=7_500_000_000, bytes_accessed=20_000_000, transcendentals=200_000),
    )(block_input, qkv_weight, grad_attn)


def solution(mesh):
    placed = (P("dp", None), P(None, None, "mp"), P("dp", "mp"))
    return jax.shard_map(
        on_device,
        mesh=mesh,
        in_specs=placed,
        out_specs=(P("dp", None), P(None, "dp", "mp")),
        check_vma=False,
    )
```

```python
import functools
import math

import jax
import jax.numpy as jnp
from jax import lax
from jax.experimental import pallas as pl
from jax.experimental.pallas import tpu as pltpu
from jax.sharding import PartitionSpec as P

MESH = pl.DeviceIdType.MESH
F32 = jnp.float32
BF16 = jnp.bfloat16
EPSILON = 1e-06

NX, NZ = 4, 8
ROWS = 256
D = 6144
HALF = D // 2
INNER = 256
HD = 128
OWN = 16
SLICE = 384
EH = 384
XROWS = 64
RZ = 1280
RY = HALF - RZ
AZ = 2048
AY = HALF - AZ
CHAINS = ((0, 0), (1, 1), (1, 0), (0, 1))
HOPS = {chain: 4 if chain[0] == chain[1] else 3 for chain in CHAINS}
FIRST = {(0, 0): 0, (1, 1): 4, (1, 0): 8, (0, 1): 11}
SLOTS = 14


def normalize(values):
    row_mean = jnp.mean(values, axis=-1, keepdims=True)
    centered = values - row_mean
    inv_std = lax.rsqrt(jnp.mean(centered * centered, axis=-1, keepdims=True) + EPSILON)
    return centered * inv_std, inv_std


def norm_back(upstream, normed, inv_std):
    mean_grad = jnp.mean(upstream, axis=-1, keepdims=True)
    mean_cross = jnp.mean(upstream * normed, axis=-1, keepdims=True)
    return inv_std * (upstream - mean_grad - normed * mean_cross)


def dot(a, b, ca, cb):
    return lax.dot_general(a, b, (((ca,), (cb,)), ((), ())), preferred_element_type=F32)


def head_grads(q, k, v, g):
    factor = 1.0 / math.sqrt(HD)
    q_hat, q_inv = normalize(q.astype(F32))
    k_hat, k_inv = normalize(k.astype(F32))
    q_low = q_hat.astype(BF16)
    k_low = k_hat.astype(BF16)
    exp_scores = jnp.exp(dot(q_low, k_low, 1, 1) * factor)
    probs = exp_scores / jnp.sum(exp_scores, axis=-1, keepdims=True)
    grad_probs = dot(g, v, 1, 1)
    grad_v = dot(probs.astype(BF16), g, 0, 0)
    row_term = jnp.sum(probs * grad_probs, axis=-1, keepdims=True)
    grad_scores = (probs * (grad_probs - row_term) * factor).astype(BF16)
    grad_q = norm_back(dot(grad_scores, k_low, 1, 0), q_hat, q_inv)
    grad_k = norm_back(dot(grad_scores, q_low, 0, 0), k_hat, k_inv)
    return grad_q, grad_k, grad_v


def kernel(
    x_hbm, w_hbm, g_hbm, og, gwv,
    xv, wv, gv, nv, pv, gp, gp2, nr, tv, zslots, yslots, yx, zf, ry, bp, rb, yb, xh, xinv,
    x_sem, w_sem, g_sem, s_sem, core_sem, z_sem, y_sem, yx_sem, ry_sem, ag_sem, az_sem, ay_sem, b_sem, by_sem,
):
    dp, mp = lax.axis_index("dp"), lax.axis_index("mp")
    x, yl, c = dp // 4, (dp // 2) % 2, dp % 2
    z, yh = mp // 2, mp % 2

    def at(x_, yl_, c_, z_, yh_):
        return ((x_ * 2 + yl_) * 2 + c_, z_ * 2 + yh_)

    to_z = (at(x, yl, c, (z + 1) % NZ, yh), at(x, yl, c, (z + NZ - 1) % NZ, yh))
    to_x = (at((x + 1) % NX, yl, c, z, yh), at((x + NX - 1) % NX, yl, c, z, yh))
    to_yh = at(x, yl, c, z, 1 - yh)
    to_yl = at(x, 1 - yl, c, z, yh)
    to_core = at(x, yl, 1 - c, z, yh)

    def x_copy(i):
        rows = pl.ds(pl.multiple_of(i * XROWS, XROWS), XROWS)
        return pltpu.make_async_copy(x_hbm.at[rows], xv.at[rows], x_sem.at[i])

    def w_copy(i):
        return pltpu.make_async_copy(w_hbm.at[i], wv.at[i], w_sem.at[i])

    g_copy = pltpu.make_async_copy(g_hbm, gv, g_sem)
    for i in range(ROWS // XROWS):
        x_copy(i).start()
    w_copy(0).start()
    g_copy.start()

    barrier = pltpu.get_barrier_semaphore()
    neighbours = to_z + to_x + (to_yh, to_yl, to_core)
    for d in neighbours:
        pl.semaphore_signal(barrier, inc=1, device_id=d, device_id_type=MESH)

    sent = [0] * 5

    def remote(src, dst, group, r, d):
        cp = pltpu.make_async_remote_copy(
            src_ref=src, dst_ref=dst, send_sem=s_sem.at[group], recv_sem=r, device_id=d, device_id_type=MESH
        )
        cp.start()
        sent[group] += math.prod(src.shape)
        return cp

    def wait_all(ref, sem):
        pltpu.make_async_copy(ref, ref, sem).wait()

    def normed_rows(i, carry):
        x_copy(i).wait()

        @pl.when(i % 2 == 1)
        def _():
            w_copy((i + 1) // 2).start()

        rows = pl.ds(pl.multiple_of(i * XROWS, XROWS), XROWS)
        shape = (XROWS, 128)
        tiles = [pl.ds(t * 128, 128) for t in range(D // 128)]
        total = jnp.zeros(shape, F32)
        for tile in tiles:
            total += xv[rows, tile].astype(F32)
        mean = jnp.broadcast_to(jnp.sum(total, axis=-1, keepdims=True) * (1.0 / D), shape)
        total = jnp.zeros(shape, F32)
        for tile in tiles:
            centered = xv[rows, tile].astype(F32) - mean
            total += centered * centered
        variance = jnp.sum(total, axis=-1, keepdims=True) * (1.0 / D)
        inv = jnp.broadcast_to(lax.rsqrt(variance + EPSILON), shape)
        for tile in tiles:
            nv[rows, tile] = ((xv[rows, tile].astype(F32) - mean) * inv).astype(BF16)
        return carry

    lax.fori_loop(0, ROWS // XROWS, normed_rows, 0)

    def project(i, carry):
        w_copy(i).wait()
        pv[:, pl.ds(pl.multiple_of(i * INNER, INNER), INNER)] = dot(nv[...], wv[i], 1, 0).astype(BF16)
        return carry

    lax.fori_loop(0, 3, project, 0)
    g_copy.wait()
    for h in range(INNER // HD):
        cols = [pl.ds(i * INNER + h * HD, HD) for i in range(3)]
        grads = head_grads(pv[:, cols[0]], pv[:, cols[1]], pv[:, cols[2]], gv[:, pl.ds(h * HD, HD)])
        for col, grad in zip(cols, grads):
            gp[:, col] = grad.astype(BF16)
    pl.semaphore_wait(barrier, len(neighbours))

    def block_rows(delta, h):
        return pl.ds(pl.multiple_of((z + delta) % NZ * 2 * OWN + h * OWN, OWN), OWN)

    def both_rows(delta):
        return pl.ds(pl.multiple_of((z + delta) % NZ * 2 * OWN, 2 * OWN), 2 * OWN)

    def ahead(way, far):
        return far if way == 0 else (NZ - far) % NZ

    rz_cols = (pl.ds(0, RZ), pl.ds(D - RZ, RZ))
    ry_cols = (pl.ds(RZ, RY), pl.ds(HALF, RY))
    ry_part = (pl.ds(0, RY), pl.ds(RY, RY))
    zs, ys, y_first = {}, {}, {}

    def z_send(chain, k, src):
        slot = FIRST[chain] + k
        zs[chain, k] = remote(src, zslots.at[slot], 0, z_sem.at[slot], to_z[chain[0]])

    def y_send(chain, k, src):
        slot = FIRST[chain] + k
        ys[chain, k] = remote(src, yslots.at[slot], 0, y_sem.at[slot], to_z[chain[0]])

    def z_start(ch):
        for way in range(2):
            chain = (way, ch)
            z_send(chain, 0, tv.at[both_rows(ahead(way, HOPS[chain])), rz_cols[ch]])

    def z_take(k):
        for chain in CHAINS:
            way, ch = chain
            far = HOPS[chain] - k - 1
            if far > 0:
                slot = FIRST[chain] + k
                own = tv[both_rows(ahead(way, far)), rz_cols[ch]].astype(F32)
                zs[chain, k].wait_recv()
                zslots[slot] = (zslots[slot].astype(F32) + own).astype(BF16)
                z_send(chain, k + 1, zslots.at[slot])

    def z_total(ch, h):
        rows = pl.ds(pl.multiple_of(h * OWN, OWN), OWN)
        total = tv[block_rows(0, h), rz_cols[ch]].astype(F32)
        for way in (1 - ch, ch):
            slot = FIRST[way, ch] + HOPS[way, ch] - 1
            total += zslots[slot, rows, :].astype(F32)
        return total

    def y_own(ch, delta):
        own = tv[block_rows(delta, yh), ry_cols[ch]].astype(F32)
        return own + yx[delta, :, ry_part[ch]].astype(F32)

    def y_start():
        for delta in (4, 3, 5):
            y_first[delta].wait_recv()
        for chain in CHAINS:
            way, ch = chain
            delta = ahead(way, HOPS[chain])
            yx[delta, :, ry_part[ch]] = y_own(ch, delta).astype(BF16)
            y_send(chain, 0, yx.at[delta, :, ry_part[ch]])

    def y_take(k):
        for way in range(2):
            far = HOPS[1 - way, way] - k - 1
            if far > 0:
                y_first[ahead(way, far)].wait_recv()
        for chain in CHAINS:
            way, ch = chain
            far = HOPS[chain] - k - 1
            if far > 0:
                slot = FIRST[chain] + k
                own = y_own(ch, ahead(way, far))
                ys[chain, k].wait_recv()
                yslots[slot] = (yslots[slot].astype(F32) + own).astype(BF16)
                y_send(chain, k + 1, yslots.at[slot])

    def y_total(ch):
        total = y_own(ch, 0)
        for way in (1 - ch, ch):
            k = HOPS[way, ch] - 1
            ys[(way, ch), k].wait_recv()
            total += yslots[FIRST[way, ch] + k].astype(F32)
        return total

    def terms(start, width):
        cols = pl.ds(start, width)
        total = dot(gp[:, pl.ds(0, INNER)], wv[0, cols, :], 1, 1)
        for j in range(1, 3):
            total += dot(gp[:, pl.ds(j * INNER, INNER)], wv[j, cols, :], 1, 1)
        tv[:, cols] = total.astype(BF16)

    def y_exchange():
        for delta in (4, 3, 5, 2, 6, 1, 7, 0):
            y_first[delta] = remote(
                tv.at[block_rows(delta, 1 - yh), pl.ds(RZ, 2 * RY)], yx.at[delta], 0, yx_sem.at[delta], to_yh
            )

    terms(0, RZ)
    z_start(0)
    terms(D - RZ, RZ)
    z_start(1)
    terms(RZ, RY)
    terms(HALF, RY)
    y_exchange()
    for i in range(8):
        cols = pl.ds(pl.multiple_of((i * 2 + 1 - c) * SLICE, 128), SLICE)
        remote(nv.at[:, cols], nr.at[:, pl.ds(i * SLICE, SLICE)], 2, core_sem.at[0], to_core)
    remote(gp, gp2, 2, core_sem.at[1], to_core)

    def b_units(j):
        ys_ = 1 - yl if j == 0 else yl

        def unit(delta, carry):
            block = (x + delta) % NX
            mine = pl.ds(pl.multiple_of(((block * 2 + ys_) * 2 + c) * SLICE, 128), SLICE)
            other = pl.ds(pl.multiple_of((block * 2 + ys_) * SLICE, 128), SLICE)
            total = dot(nv[:, mine], gp[...], 0, 0) + dot(nr[:, other], gp2[...], 0, 0)
            for ch in range(2):
                bp[j, delta, ch] = total[:, ch * EH : (ch + 1) * EH].astype(BF16)
            return carry

        lax.fori_loop(0, NX, unit, 0)

    def b_send(way, kind, j, src):
        remote(src, rb.at[j, kind, way], 3 + j, b_sem.at[j, 0 if kind == 0 else 1], to_x[way])

    def b_start(j):
        for way in range(2):
            b_send(way, 0, j, bp.at[j, 2, way])
        for way in range(2):
            b_send(way, 1, j, bp.at[j, 1 if way == 0 else 3, 1 - way])

    def b_take(j):
        wait_all(rb.at[j, 0], b_sem.at[j, 0])
        for way in range(2):
            own = bp[j, 1 if way == 0 else 3, way].astype(F32)
            rb[j, 0, way] = (rb[j, 0, way].astype(F32) + own).astype(BF16)
            b_send(way, 2, j, rb.at[j, 0, way])

    def b_total(ch, j):
        total = bp[j, 0, ch].astype(F32) + rb[j, 1, 1 - ch].astype(F32)
        return total + rb[j, 2, ch].astype(F32)

    own_rows = block_rows(0, yh)
    hat, inv = normalize(xv[own_rows, :].astype(F32))
    xh[...] = hat
    xinv[...] = jnp.broadcast_to(inv, xinv.shape)
    wait_all(nr, core_sem.at[0])
    wait_all(gp2, core_sem.at[1])
    b_units(0)
    b_start(0)
    z_take(0)
    y_start()
    b_units(1)
    z_take(1)
    y_take(0)
    b_take(0)
    b_start(1)
    z_take(2)
    y_take(1)
    for chain in CHAINS:
        zs[chain, HOPS[chain] - 1].wait_recv()
    for ch in range(2):
        zf[:, pl.ds(ch * RZ, RZ)] = z_total(ch, 1 - yh).astype(BF16)
    y = remote(zf, ry, 0, ry_sem, to_yh)
    y_take(2)
    totals = [[z_total(ch, yh)] for ch in range(2)]
    y_first[0].wait_recv()
    for ch in range(2):
        totals[ch].append(y_total(ch))
    y.wait_recv()
    for ch in range(2):
        totals[ch][0] += ry[:, pl.ds(ch * RZ, RZ)].astype(F32)
    grad_normed = jnp.concatenate(totals[0] + totals[1][::-1], axis=1)
    og[own_rows, :] = norm_back(grad_normed, xh[...], xinv[:, :1]).astype(BF16)

    ag, az = {}, {}
    ag_cols = ((pl.ds(0, HALF), pl.ds(0, AZ)), (pl.ds(HALF, HALF), pl.ds(D - AZ, AZ)))
    ay_cols = pl.ds(AZ, 2 * AY)

    def ag_send(chain, k, u):
        way, ch = chain
        part = og.at[block_rows(ahead(1 - way, k), yh if u == 0 else 1 - yh), ag_cols[ch][u]]
        ag[chain, k, u] = remote(part, part, 1, ag_sem.at[u, FIRST[chain] + k], to_z[way])

    def ay_send(delta):
        part = og.at[block_rows(delta, yh), ay_cols]
        remote(part, part, 1, ay_sem, to_yh)

    def ag_take(k):
        for u in range(2):
            for chain in CHAINS:
                if k < HOPS[chain]:
                    ag[chain, k, u].wait_recv()
                    if k + 1 < HOPS[chain]:
                        ag_send(chain, k + 1, u)
            if u == 0:
                for delta in {ahead(1 - way, k + 1) for way in range(2)}:
                    ay_send(delta)

    for ch in range(2):
        part = og.at[own_rows, ag_cols[ch][1]]
        az[ch] = remote(part, part, 1, az_sem.at[ch], to_yh)
    for chain in CHAINS:
        ag_send(chain, 0, 0)
    ay_send(0)
    for ch in range(2):
        az[ch].wait_recv()
        for way in range(2):
            ag_send((way, ch), 0, 1)
    wait_all(rb.at[0, pl.ds(1, 2)], b_sem.at[0, 1])
    for ch in range(2):
        rb[0, 2, ch] = b_total(ch, 0).astype(BF16)
    by = remote(rb.at[0, 2], yb, 3, by_sem, to_yl)
    ag_take(0)
    b_take(1)
    ag_take(1)
    ag_take(2)
    wait_all(rb.at[1, pl.ds(1, 2)], b_sem.at[1, 1])
    by.wait_recv()
    for ch in range(2):
        total = (b_total(ch, 1) + yb[ch].astype(F32)).astype(BF16)
        if ch == 0:
            gwv[0, :, :] = total[:, :256]
            gwv[1, :, :128] = total[:, 256:]
        else:
            gwv[1, :, 128:] = total[:, :128]
            gwv[2, :, :] = total[:, 128:]
    ag_take(3)
    wait_all(og.at[pl.ds(0, ROWS // 2), ay_cols], ay_sem)
    for group, count in enumerate(sent):
        wait_all(wv.at[0, pl.ds(0, count // INNER)], s_sem.at[group])


def on_device(block_input, qkv_weight, grad_attn):
    dma = pltpu.SemaphoreType.DMA
    vmem = pl.BlockSpec(memory_space=pltpu.VMEM)
    return pl.pallas_call(
        kernel,
        out_shape=(pltpu.VMEM((ROWS, D), BF16), pltpu.VMEM((3, SLICE, INNER), BF16)),
        in_specs=[pl.BlockSpec(memory_space=pl.ANY)] * 3,
        out_specs=(vmem, vmem),
        scratch_shapes=[
            pltpu.VMEM((ROWS, D), BF16),
            pltpu.VMEM((3, D, INNER), BF16),
            pltpu.VMEM((ROWS, INNER), BF16),
            pltpu.VMEM((ROWS, D), BF16),
            pltpu.VMEM((ROWS, 3 * INNER), BF16),
            pltpu.VMEM((ROWS, 3 * INNER), BF16),
            pltpu.VMEM((ROWS, 3 * INNER), BF16),
            pltpu.VMEM((ROWS, HALF), BF16),
            pltpu.VMEM((ROWS, D), BF16),
            pltpu.VMEM((SLOTS, 2 * OWN, RZ), BF16),
            pltpu.VMEM((SLOTS, OWN, RY), BF16),
            pltpu.VMEM((NZ, OWN, 2 * RY), BF16),
            pltpu.VMEM((OWN, 2 * RZ), BF16),
            pltpu.VMEM((OWN, 2 * RZ), BF16),
            pltpu.VMEM((2, NX, 2, SLICE, EH), BF16),
            pltpu.VMEM((2, 3, 2, SLICE, EH), BF16),
            pltpu.VMEM((2, SLICE, EH), BF16),
            pltpu.VMEM((OWN, D), F32),
            pltpu.VMEM((OWN, 128), F32),
            dma((ROWS // XROWS,)), dma((3,)), dma(()), dma((5,)),
            dma((2,)), dma((SLOTS,)), dma((SLOTS,)), dma((NZ,)), dma(()),
            dma((2, SLOTS)), dma((2,)), dma(()), dma((2, 2)), dma(()),
        ],
        compiler_params=pltpu.CompilerParams(
            collective_id=0, has_side_effects=True, vmem_limit_bytes=54 * 2**20
        ),
        cost_estimate=pl.CostEstimate(flops=7_500_000_000, bytes_accessed=20_000_000, transcendentals=200_000),
    )(block_input, qkv_weight, grad_attn)


def solution(mesh):
    placed = (P("dp", None), P(None, None, "mp"), P("dp", "mp"))
    return jax.shard_map(
        on_device,
        mesh=mesh,
        in_specs=placed,
        out_specs=(P("dp", None), P(None, "dp", "mp")),
        check_vma=False,
    )
```

```python
import functools
import math

import jax
import jax.numpy as jnp
from jax import lax
from jax.experimental import pallas as pl
from jax.experimental.pallas import tpu as pltpu
from jax.sharding import PartitionSpec as P

MESH = pl.DeviceIdType.MESH
F32 = jnp.float32
BF16 = jnp.bfloat16
EPSILON = 1e-06

NX, NZ = 4, 8
ROWS = 256
D = 6144
HALF = D // 2
INNER = 256
HD = 128
OWN = 16
SLICE = 384
EH = 384
XROWS = 64
RZ = 1408
RY = HALF - RZ
AZ = 2048
AY = HALF - AZ
CHAINS = ((0, 0), (1, 1), (1, 0), (0, 1))
HOPS = {chain: 4 if chain[0] == chain[1] else 3 for chain in CHAINS}
FIRST = {(0, 0): 0, (1, 1): 4, (1, 0): 8, (0, 1): 11}
SLOTS = 14


def normalize(values):
    row_mean = jnp.mean(values, axis=-1, keepdims=True)
    centered = values - row_mean
    inv_std = lax.rsqrt(jnp.mean(centered * centered, axis=-1, keepdims=True) + EPSILON)
    return centered * inv_std, inv_std


def norm_back(upstream, normed, inv_std):
    mean_grad = jnp.mean(upstream, axis=-1, keepdims=True)
    mean_cross = jnp.mean(upstream * normed, axis=-1, keepdims=True)
    return inv_std * (upstream - mean_grad - normed * mean_cross)


def dot(a, b, ca, cb):
    return lax.dot_general(a, b, (((ca,), (cb,)), ((), ())), preferred_element_type=F32)


def head_grads(q, k, v, g):
    factor = 1.0 / math.sqrt(HD)
    q_hat, q_inv = normalize(q.astype(F32))
    k_hat, k_inv = normalize(k.astype(F32))
    q_low = q_hat.astype(BF16)
    k_low = k_hat.astype(BF16)
    exp_scores = jnp.exp(dot(q_low, k_low, 1, 1) * factor)
    probs = exp_scores / jnp.sum(exp_scores, axis=-1, keepdims=True)
    grad_probs = dot(g, v, 1, 1)
    grad_v = dot(probs.astype(BF16), g, 0, 0)
    row_term = jnp.sum(probs * grad_probs, axis=-1, keepdims=True)
    grad_scores = (probs * (grad_probs - row_term) * factor).astype(BF16)
    grad_q = norm_back(dot(grad_scores, k_low, 1, 0), q_hat, q_inv)
    grad_k = norm_back(dot(grad_scores, q_low, 0, 0), k_hat, k_inv)
    return grad_q, grad_k, grad_v


def kernel(
    x_hbm, w_hbm, g_hbm, og, gwv,
    xv, wv, gv, nv, pv, gp, gp2, nr, tv, zslots, yslots, yx, zf, ry, bp, rb, yb, xh, xinv,
    x_sem, w_sem, g_sem, s_sem, core_sem, z_sem, y_sem, yx_sem, ry_sem, ag_sem, az_sem, ay_sem, b_sem, by_sem,
):
    dp, mp = lax.axis_index("dp"), lax.axis_index("mp")
    x, yl, c = dp // 4, (dp // 2) % 2, dp % 2
    z, yh = mp // 2, mp % 2

    def at(x_, yl_, c_, z_, yh_):
        return ((x_ * 2 + yl_) * 2 + c_, z_ * 2 + yh_)

    to_z = (at(x, yl, c, (z + 1) % NZ, yh), at(x, yl, c, (z + NZ - 1) % NZ, yh))
    to_x = (at((x + 1) % NX, yl, c, z, yh), at((x + NX - 1) % NX, yl, c, z, yh))
    to_yh = at(x, yl, c, z, 1 - yh)
    to_yl = at(x, 1 - yl, c, z, yh)
    to_core = at(x, yl, 1 - c, z, yh)

    def x_copy(i):
        rows = pl.ds(pl.multiple_of(i * XROWS, XROWS), XROWS)
        return pltpu.make_async_copy(x_hbm.at[rows], xv.at[rows], x_sem.at[i])

    def w_copy(i):
        return pltpu.make_async_copy(w_hbm.at[i], wv.at[i], w_sem.at[i])

    g_copy = pltpu.make_async_copy(g_hbm, gv, g_sem)
    for i in range(ROWS // XROWS):
        x_copy(i).start()
    w_copy(0).start()
    g_copy.start()

    barrier = pltpu.get_barrier_semaphore()
    neighbours = to_z + to_x + (to_yh, to_yl, to_core)
    for d in neighbours:
        pl.semaphore_signal(barrier, inc=1, device_id=d, device_id_type=MESH)

    sent = [0] * 5

    def remote(src, dst, group, r, d):
        cp = pltpu.make_async_remote_copy(
            src_ref=src, dst_ref=dst, send_sem=s_sem.at[group], recv_sem=r, device_id=d, device_id_type=MESH
        )
        cp.start()
        sent[group] += math.prod(src.shape)
        return cp

    def wait_all(ref, sem):
        pltpu.make_async_copy(ref, ref, sem).wait()

    def normed_rows(i, carry):
        x_copy(i).wait()

        @pl.when(i % 2 == 1)
        def _():
            w_copy((i + 1) // 2).start()

        rows = pl.ds(pl.multiple_of(i * XROWS, XROWS), XROWS)
        shape = (XROWS, 128)
        tiles = [pl.ds(t * 128, 128) for t in range(D // 128)]
        total = jnp.zeros(shape, F32)
        for tile in tiles:
            total += xv[rows, tile].astype(F32)
        mean = jnp.broadcast_to(jnp.sum(total, axis=-1, keepdims=True) * (1.0 / D), shape)
        total = jnp.zeros(shape, F32)
        for tile in tiles:
            centered = xv[rows, tile].astype(F32) - mean
            total += centered * centered
        variance = jnp.sum(total, axis=-1, keepdims=True) * (1.0 / D)
        inv = jnp.broadcast_to(lax.rsqrt(variance + EPSILON), shape)
        for tile in tiles:
            nv[rows, tile] = ((xv[rows, tile].astype(F32) - mean) * inv).astype(BF16)
        return carry

    lax.fori_loop(0, ROWS // XROWS, normed_rows, 0)

    pl.semaphore_wait(barrier, len(neighbours))
    for i in range(8):
        cols = pl.ds(pl.multiple_of((i * 2 + 1 - c) * SLICE, 128), SLICE)
        remote(nv.at[:, cols], nr.at[:, pl.ds(i * SLICE, SLICE)], 2, core_sem.at[0], to_core)

    def project(i, carry):
        w_copy(i).wait()
        pv[:, pl.ds(pl.multiple_of(i * INNER, INNER), INNER)] = dot(nv[...], wv[i], 1, 0).astype(BF16)
        return carry

    lax.fori_loop(0, 3, project, 0)
    g_copy.wait()
    for h in range(INNER // HD):
        cols = [pl.ds(i * INNER + h * HD, HD) for i in range(3)]
        grads = head_grads(pv[:, cols[0]], pv[:, cols[1]], pv[:, cols[2]], gv[:, pl.ds(h * HD, HD)])
        for col, grad in zip(cols, grads):
            gp[:, col] = grad.astype(BF16)
    remote(gp, gp2, 2, core_sem.at[1], to_core)

    def block_rows(delta, h):
        return pl.ds(pl.multiple_of((z + delta) % NZ * 2 * OWN + h * OWN, OWN), OWN)

    def both_rows(delta):
        return pl.ds(pl.multiple_of((z + delta) % NZ * 2 * OWN, 2 * OWN), 2 * OWN)

    def ahead(way, far):
        return far if way == 0 else (NZ - far) % NZ

    rz_cols = (pl.ds(0, RZ), pl.ds(D - RZ, RZ))
    ry_cols = (pl.ds(RZ, RY), pl.ds(HALF, RY))
    ry_part = (pl.ds(0, RY), pl.ds(RY, RY))
    zs, ys, y_first = {}, {}, {}

    def z_send(chain, k, src):
        slot = FIRST[chain] + k
        zs[chain, k] = remote(src, zslots.at[slot], 0, z_sem.at[slot], to_z[chain[0]])

    def y_send(chain, k, src):
        slot = FIRST[chain] + k
        ys[chain, k] = remote(src, yslots.at[slot], 0, y_sem.at[slot], to_z[chain[0]])

    def z_start(ch):
        for way in range(2):
            chain = (way, ch)
            z_send(chain, 0, tv.at[both_rows(ahead(way, HOPS[chain])), rz_cols[ch]])

    def z_take(k):
        for chain in CHAINS:
            way, ch = chain
            far = HOPS[chain] - k - 1
            if far > 0:
                slot = FIRST[chain] + k
                own = tv[both_rows(ahead(way, far)), rz_cols[ch]].astype(F32)
                zs[chain, k].wait_recv()
                zslots[slot] = (zslots[slot].astype(F32) + own).astype(BF16)
                z_send(chain, k + 1, zslots.at[slot])

    def z_total(ch, h):
        rows = pl.ds(pl.multiple_of(h * OWN, OWN), OWN)
        total = tv[block_rows(0, h), rz_cols[ch]].astype(F32)
        for way in (1 - ch, ch):
            slot = FIRST[way, ch] + HOPS[way, ch] - 1
            total += zslots[slot, rows, :].astype(F32)
        return total

    def y_own(ch, delta):
        own = tv[block_rows(delta, yh), ry_cols[ch]].astype(F32)
        return own + yx[delta, :, ry_part[ch]].astype(F32)

    def y_start():
        for delta in (4, 3, 5):
            y_first[delta].wait_recv()
        for chain in CHAINS:
            way, ch = chain
            delta = ahead(way, HOPS[chain])
            yx[delta, :, ry_part[ch]] = y_own(ch, delta).astype(BF16)
            y_send(chain, 0, yx.at[delta, :, ry_part[ch]])

    def y_take(k):
        for way in range(2):
            far = HOPS[1 - way, way] - k - 1
            if far > 0:
                y_first[ahead(way, far)].wait_recv()
        for chain in CHAINS:
            way, ch = chain
            far = HOPS[chain] - k - 1
            if far > 0:
                slot = FIRST[chain] + k
                own = y_own(ch, ahead(way, far))
                ys[chain, k].wait_recv()
                yslots[slot] = (yslots[slot].astype(F32) + own).astype(BF16)
                y_send(chain, k + 1, yslots.at[slot])

    def y_total(ch):
        total = y_own(ch, 0)
        for way in (1 - ch, ch):
            k = HOPS[way, ch] - 1
            ys[(way, ch), k].wait_recv()
            total += yslots[FIRST[way, ch] + k].astype(F32)
        return total

    def terms(start, width):
        cols = pl.ds(start, width)
        total = dot(gp[:, pl.ds(0, INNER)], wv[0, cols, :], 1, 1)
        for j in range(1, 3):
            total += dot(gp[:, pl.ds(j * INNER, INNER)], wv[j, cols, :], 1, 1)
        tv[:, cols] = total.astype(BF16)

    def y_exchange():
        for delta in (4, 3, 5, 2, 6, 1, 7, 0):
            y_first[delta] = remote(
                tv.at[block_rows(delta, 1 - yh), pl.ds(RZ, 2 * RY)], yx.at[delta], 0, yx_sem.at[delta], to_yh
            )

    terms(RZ, 2 * RY)
    y_exchange()
    terms(0, RZ)
    z_start(0)
    terms(D - RZ, RZ)
    z_start(1)

    def b_units(j):
        ys_ = 1 - yl if j == 0 else yl

        def unit(delta, carry):
            block = (x + delta) % NX
            mine = pl.ds(pl.multiple_of(((block * 2 + ys_) * 2 + c) * SLICE, 128), SLICE)
            other = pl.ds(pl.multiple_of((block * 2 + ys_) * SLICE, 128), SLICE)
            total = dot(nv[:, mine], gp[...], 0, 0) + dot(nr[:, other], gp2[...], 0, 0)
            for ch in range(2):
                bp[j, delta, ch] = total[:, ch * EH : (ch + 1) * EH].astype(BF16)
            return carry

        lax.fori_loop(0, NX, unit, 0)

    def b_send(way, kind, j, src):
        remote(src, rb.at[j, kind, way], 3 + j, b_sem.at[j, 0 if kind == 0 else 1], to_x[way])

    def b_start(j):
        for way in range(2):
            b_send(way, 0, j, bp.at[j, 2, way])
        for way in range(2):
            b_send(way, 1, j, bp.at[j, 1 if way == 0 else 3, 1 - way])

    def b_take(j):
        wait_all(rb.at[j, 0], b_sem.at[j, 0])
        for way in range(2):
            own = bp[j, 1 if way == 0 else 3, way].astype(F32)
            rb[j, 0, way] = (rb[j, 0, way].astype(F32) + own).astype(BF16)
            b_send(way, 2, j, rb.at[j, 0, way])

    def b_total(ch, j):
        total = bp[j, 0, ch].astype(F32) + rb[j, 1, 1 - ch].astype(F32)
        return total + rb[j, 2, ch].astype(F32)

    wait_all(nr, core_sem.at[0])
    wait_all(gp2, core_sem.at[1])
    b_units(0)
    b_start(0)
    z_take(0)
    own_rows = block_rows(0, yh)
    hat, inv = normalize(xv[own_rows, :].astype(F32))
    xh[...] = hat
    xinv[...] = jnp.broadcast_to(inv, xinv.shape)
    y_start()
    b_units(1)
    z_take(1)
    b_take(0)
    b_start(1)
    y_take(0)
    z_take(2)
    y_take(1)
    for chain in CHAINS:
        zs[chain, HOPS[chain] - 1].wait_recv()
    for ch in range(2):
        zf[:, pl.ds(ch * RZ, RZ)] = z_total(ch, 1 - yh).astype(BF16)
    y = remote(zf, ry, 0, ry_sem, to_yh)
    y_take(2)
    totals = [[z_total(ch, yh)] for ch in range(2)]
    y_first[0].wait_recv()
    for ch in range(2):
        totals[ch].append(y_total(ch))
    y.wait_recv()
    for ch in range(2):
        totals[ch][0] += ry[:, pl.ds(ch * RZ, RZ)].astype(F32)
    grad_normed = jnp.concatenate(totals[0] + totals[1][::-1], axis=1)
    og[own_rows, :] = norm_back(grad_normed, xh[...], xinv[:, :1]).astype(BF16)

    ag, az = {}, {}
    ag_cols = ((pl.ds(0, HALF), pl.ds(0, AZ)), (pl.ds(HALF, HALF), pl.ds(D - AZ, AZ)))
    ay_cols = pl.ds(AZ, 2 * AY)

    def ag_send(chain, k, u):
        way, ch = chain
        part = og.at[block_rows(ahead(1 - way, k), yh if u == 0 else 1 - yh), ag_cols[ch][u]]
        ag[chain, k, u] = remote(part, part, 1, ag_sem.at[u, FIRST[chain] + k], to_z[way])

    def ay_send(delta):
        part = og.at[block_rows(delta, yh), ay_cols]
        remote(part, part, 1, ay_sem, to_yh)

    def ag_take(k):
        for u in range(2):
            for chain in CHAINS:
                if k < HOPS[chain]:
                    ag[chain, k, u].wait_recv()
                    if k + 1 < HOPS[chain]:
                        ag_send(chain, k + 1, u)
            if u == 0:
                for delta in {ahead(1 - way, k + 1) for way in range(2)}:
                    ay_send(delta)

    for ch in range(2):
        part = og.at[own_rows, ag_cols[ch][1]]
        az[ch] = remote(part, part, 1, az_sem.at[ch], to_yh)
    for chain in CHAINS:
        ag_send(chain, 0, 0)
    ay_send(0)
    for ch in range(2):
        az[ch].wait_recv()
        for way in range(2):
            ag_send((way, ch), 0, 1)
    wait_all(rb.at[0, pl.ds(1, 2)], b_sem.at[0, 1])
    for ch in range(2):
        rb[0, 2, ch] = b_total(ch, 0).astype(BF16)
    by = remote(rb.at[0, 2], yb, 3, by_sem, to_yl)
    ag_take(0)
    b_take(1)
    ag_take(1)
    ag_take(2)
    wait_all(rb.at[1, pl.ds(1, 2)], b_sem.at[1, 1])
    by.wait_recv()
    for ch in range(2):
        total = (b_total(ch, 1) + yb[ch].astype(F32)).astype(BF16)
        if ch == 0:
            gwv[0, :, :] = total[:, :256]
            gwv[1, :, :128] = total[:, 256:]
        else:
            gwv[1, :, 128:] = total[:, :128]
            gwv[2, :, :] = total[:, 128:]
    ag_take(3)
    wait_all(og.at[pl.ds(0, ROWS // 2), ay_cols], ay_sem)
    for group, count in enumerate(sent):
        wait_all(wv.at[0, pl.ds(0, count // INNER)], s_sem.at[group])


def on_device(block_input, qkv_weight, grad_attn):
    dma = pltpu.SemaphoreType.DMA
    vmem = pl.BlockSpec(memory_space=pltpu.VMEM)
    return pl.pallas_call(
        kernel,
        out_shape=(pltpu.VMEM((ROWS, D), BF16), pltpu.VMEM((3, SLICE, INNER), BF16)),
        in_specs=[pl.BlockSpec(memory_space=pl.ANY)] * 3,
        out_specs=(vmem, vmem),
        scratch_shapes=[
            pltpu.VMEM((ROWS, D), BF16),
            pltpu.VMEM((3, D, INNER), BF16),
            pltpu.VMEM((ROWS, INNER), BF16),
            pltpu.VMEM((ROWS, D), BF16),
            pltpu.VMEM((ROWS, 3 * INNER), BF16),
            pltpu.VMEM((ROWS, 3 * INNER), BF16),
            pltpu.VMEM((ROWS, 3 * INNER), BF16),
            pltpu.VMEM((ROWS, HALF), BF16),
            pltpu.VMEM((ROWS, D), BF16),
            pltpu.VMEM((SLOTS, 2 * OWN, RZ), BF16),
            pltpu.VMEM((SLOTS, OWN, RY), BF16),
            pltpu.VMEM((NZ, OWN, 2 * RY), BF16),
            pltpu.VMEM((OWN, 2 * RZ), BF16),
            pltpu.VMEM((OWN, 2 * RZ), BF16),
            pltpu.VMEM((2, NX, 2, SLICE, EH), BF16),
            pltpu.VMEM((2, 3, 2, SLICE, EH), BF16),
            pltpu.VMEM((2, SLICE, EH), BF16),
            pltpu.VMEM((OWN, D), F32),
            pltpu.VMEM((OWN, 128), F32),
            dma((ROWS // XROWS,)), dma((3,)), dma(()), dma((5,)),
            dma((2,)), dma((SLOTS,)), dma((SLOTS,)), dma((NZ,)), dma(()),
            dma((2, SLOTS)), dma((2,)), dma(()), dma((2, 2)), dma(()),
        ],
        compiler_params=pltpu.CompilerParams(
            collective_id=0, has_side_effects=True, vmem_limit_bytes=54 * 2**20
        ),
        cost_estimate=pl.CostEstimate(flops=7_500_000_000, bytes_accessed=20_000_000, transcendentals=200_000),
    )(block_input, qkv_weight, grad_attn)


def solution(mesh):
    placed = (P("dp", None), P(None, None, "mp"), P("dp", "mp"))
    return jax.shard_map(
        on_device,
        mesh=mesh,
        in_specs=placed,
        out_specs=(P("dp", None), P(None, "dp", "mp")),
        check_vma=False,
    )
```
